32 devices in a mesh: shard: 4 (over y, core), ctx: 4 (over z), tp: 2 (over x).
Axes of the slice: x: 2, y: 2, z: 4, core: 2. Of those that a mesh axis runs over, the one named last changes fastest.
Arguments:
- tokens: bfloat16 [4, 2048, 1024], P('shard', 'ctx'), may hold values from -6 to 6
- gain_attn: bfloat16 [1024], replicated, may hold values from 0.25 to 1.75
- gain_moe: bfloat16 [1024], replicated, may hold values from 0.25 to 1.75
- query_weight: bfloat16 [1024, 1024], P('shard', 'tp'), may hold values from -0.1875 to 0.1875
- key_weight: bfloat16 [1024, 512], P('shard', 'tp'), may hold values from -0.1875 to 0.1875
- value_weight: bfloat16 [1024, 512], P('shard', 'tp'), may hold values from -0.1875 to 0.1875
- out_weight: bfloat16 [1024, 1024], P('tp', 'shard'), may hold values from -3 to 3
- router_weight: bfloat16 [1024, 16], P('shard'), may hold values from -0.09375 to 0.09375
- gate_weight: bfloat16 [16, 1024, 512], P(None, 'shard', 'tp'), may hold values from -0.1875 to 0.1875
- up_weight: bfloat16 [16, 1024, 512], P(None, 'shard', 'tp'), may hold values from -0.1875 to 0.1875
- down_weight: bfloat16 [16, 512, 1024], P(None, 'tp', 'shard'), may hold values from -1 to 1
- expert_routes: int32 [4, 2048, 8], P('shard', 'ctx'), may hold values from 0 to 15, all different within a row; in each aligned block of 512 rows (0 to 511, 512 to 1023, ..., all dimensions but the last counted through in order) at most 320 rows name the same one
- cotangent: bfloat16 [4, 2048, 1024], P('shard', 'ctx'), may hold values from -6 to 6
Outputs:
- output: bfloat16 [4, 2048, 1024], P('shard', 'ctx')
- grad_tokens: bfloat16 [4, 2048, 1024], P('shard', 'ctx')
- grad_gain_attn: float32 [1024], P(('shard', 'ctx'))
- grad_gain_moe: float32 [1024], P(('shard', 'ctx'))
- grad_query_weight: float32 [1024, 1024], P(('shard', 'ctx'), 'tp')
- grad_key_weight: float32 [1024, 512], P(('shard', 'ctx'), 'tp')
- grad_value_weight: float32 [1024, 512], P(('shard', 'ctx'), 'tp')
- grad_out_weight: float32 [1024, 1024], P('tp', ('shard', 'ctx'))
- grad_router_weight: float32 [1024, 16], P(('shard', 'ctx'))
- grad_gate_weight: float32 [16, 1024, 512], P(None, ('shard', 'ctx'), 'tp')
- grad_up_weight: float32 [16, 1024, 512], P(None, ('shard', 'ctx'), 'tp')
- grad_down_weight: float32 [16, 512, 1024], P(None, 'tp', ('shard', 'ctx'))
The draws below stay inside these ranges and needn't reach their ends.
Inputs may be any that keep to these rules, and one draw needn't show every extreme that they name: `expert_routes`: each row names 8 different experts; in each aligned block of 512 rows of a sequence (the rows of one device) no expert is named by more than 320 rows, a bound that some block reaches.
All inputs are finite; a program needn't handle non-finite values.
Results may differ from the reference program's by a relative error of at most 0.023.
Values may be sent and summed in bfloat16 or wider, within the bound.
A program may use at most 384 MiB of HBM per device.

```python
import math
import jax
import jax.numpy as jnp
import numpy as np
from jax import lax

D = 1024
HEADS = 16
KVH = 8
HD = 64
FF = 512
TOPK = 8
EXPERTS = 16
LEN = 2048
SEQS = 4
TOK_DEV = 512
HQ = 1024
HK = 512
CAP = 320


def spiked(array, rng, source, target, shards_of, factor):
    def block_of(axis_at):
        return (jnp.arange(array.shape[axis_at]) // (array.shape[axis_at] // shards_of)).reshape((-1,) + (1,) * (array.ndim - 1 - axis_at))

    one_side = jax.random.permutation(rng, shards_of)[block_of(target)]
    second = (block_of(target) + shards_of // 2) % shards_of
    return jnp.where((block_of(source) == one_side) | (block_of(source) == second), factor * array, array)


def shard_levels(own_key, extent, split, least, top_value):
    level = 1.0
    for dim, shards_of in split:
        draws = jax.random.uniform(jax.random.fold_in(jax.random.fold_in(own_key, 6), dim), (shards_of,), jnp.float32, least / len(split), top_value / len(split))
        level = level * jnp.repeat(jnp.exp(draws), extent[dim] // shards_of).reshape((-1,) + (1,) * (len(extent) - 1 - dim))
    return level


def routed_block(stream_key, own, number, rows, count, top, limit, skew):
    order = jax.random.permutation(stream_key, count)
    crowded, common = load_shares(count, rows * top, limit, skew, True), load_shares(count, rows * top, limit, skew, False)
    places = jnp.arange(count)

    def named(sizes, rotation):
        used = int((sizes > 0).sum())
        fixed = max(1, used // 4)
        moved = fixed + (places - fixed + rotation * (used - fixed)) % max(1, count - fixed)
        return jnp.zeros((count,), jnp.int32).at[order[jnp.where(places < fixed, places, moved)]].set(jnp.asarray(sizes, jnp.int32))

    sizes = jnp.where(number % 4 == 0, named(crowded, number // 4), named(common, number - number // 4 - 1))
    mixed = jax.random.permutation(jax.random.fold_in(own, 3), count)
    giver, receiver = mixed[0:count // 2 * 2:2], mixed[1:count // 2 * 2:2]
    room = jnp.minimum(sizes[giver] - 1, limit - sizes[receiver]) // 2
    room = jnp.where((giver == order[0]) | (receiver == order[0]) | (sizes[receiver] == 0), 0, jnp.maximum(room, 0))
    moved = jax.random.randint(jax.random.fold_in(own, 4), (count // 2,), 0, 1 << 20) % (room + 1)
    sizes = sizes.at[giver].add(-moved).at[receiver].add(moved)
    labels = jnp.searchsorted(jnp.cumsum(sizes), jnp.arange(rows * top), side="right").astype(jnp.int32)
    table = labels.reshape(top, rows).T
    table = table[jax.random.permutation(jax.random.fold_in(own, 1), rows)]
    rotation = jax.random.randint(jax.random.fold_in(own, 2), (rows, 1), 0, top)
    return jnp.take_along_axis(table, (jnp.arange(top)[None, :] + rotation) % top, axis=1)


def load_shares(amount, total, limit, slope, full):
    weights = [(1 << 20) // math.isqrt(standing ** slope) + 1 for standing in range(1, amount + 1)]
    largest = limit if full else min(limit, max(-(-total // amount), total * weights[0] // sum(weights)))
    least = 1 if total - largest >= amount - 1 else 0
    given, rest = [largest] + [least] * (amount - 1), total - largest - least * (amount - 1)
    while rest > 0:
        movable = [i for i in range(1, amount) if given[i] < largest] or [i for i in range(1, amount) if given[i] < limit]
        whole, budget = sum([weights[i] for i in movable]), rest
        for i in movable:
            extra = min(limit - given[i], max(1, budget * weights[i] // whole), rest)
            given[i] = given[i] + extra
            rest = rest - extra
    return np.array(given)


def gaussian(rng, extent, width, reach, shards=(), held_as=jnp.bfloat16):
    array = width * jax.random.normal(rng, extent, jnp.float32)
    if shards:
        array = array * shard_levels(rng, extent, shards, -0.22, 0.18)
    return jnp.clip(array, -reach, reach).astype(held_as)


def noise_with(stream_key, extent, width, limit, shards, heavy, held_as=jnp.bfloat16):
    values = width * jax.random.normal(stream_key, extent, jnp.float32)
    if shards:
        values = values * shard_levels(stream_key, extent, shards, -0.22, 0.18)
    return jnp.clip(spiked(values, jax.random.fold_in(stream_key, 3), *heavy), -limit, limit).astype(held_as)


def setup_inputs(seed: int = 0) -> dict:
    key_of = jax.random.split(jax.random.key(seed), 14)
    tokens = gaussian(key_of[0], (SEQS, LEN, D), 1.0, 6.0, ((0, 4), (1, 4)))
    gain_attn = jnp.clip(1.0 + 0.15 * jax.random.normal(key_of[1], (D,), jnp.float32), 0.25, 1.75).astype(jnp.bfloat16)
    gain_moe = jnp.clip(1.0 + 0.15 * jax.random.normal(key_of[2], (D,), jnp.float32), 0.25, 1.75).astype(jnp.bfloat16)
    query_weight = gaussian(key_of[3], (D, HQ), D ** -0.5, 0.1875, ((0, 4), (1, 2)))
    key_weight = gaussian(key_of[4], (D, HK), D ** -0.5, 0.1875, ((0, 4), (1, 2)))
    value_weight = gaussian(key_of[5], (D, HK), D ** -0.5, 0.1875, ((0, 4), (1, 2)))
    out_weight = gaussian(key_of[6], (HQ, D), 4 ** -0.5, 3.0, ((0, 2), (1, 4)))
    router_weight = gaussian(key_of[7], (D, EXPERTS), (4 * D) ** -0.5, 0.09375, ((0, 4),))
    gate_weight = gaussian(key_of[8], (EXPERTS, D, FF), D ** -0.5, 0.1875, ((1, 4), (2, 2)))
    up_weight = gaussian(key_of[9], (EXPERTS, D, FF), D ** -0.5, 0.1875, ((1, 4), (2, 2)))
    down_weight = gaussian(key_of[10], (EXPERTS, FF, D), (FF // 16) ** -0.5, 1.0, ((1, 2), (2, 4)))
    expert_routes_keys = jax.random.split(jax.random.fold_in(key_of[11], 1), SEQS * LEN // TOK_DEV)
    expert_routes_turns = jax.random.permutation(jax.random.fold_in(key_of[11], 3), SEQS * LEN // TOK_DEV)
    expert_routes = jax.vmap(lambda own, number: routed_block(jax.random.fold_in(key_of[11], 2), own, number, TOK_DEV, EXPERTS, TOPK, CAP, 1))(expert_routes_keys, expert_routes_turns).reshape((SEQS, LEN, TOPK))
    cotangent = noise_with(key_of[12], (SEQS, LEN, D), 1.0, 6.0, ((0, 4), (1, 4)), (1, 2, 4, 2.0))
    return dict(tokens=tokens, gain_attn=gain_attn, gain_moe=gain_moe, query_weight=query_weight, key_weight=key_weight, value_weight=value_weight, out_weight=out_weight, router_weight=router_weight, gate_weight=gate_weight, up_weight=up_weight, down_weight=down_weight, expert_routes=expert_routes, cotangent=cotangent)


@jax.custom_vjp
def low(v):
    return lax.optimization_barrier(v.astype(jnp.bfloat16)).astype(jnp.float32)

@jax.custom_vjp
def low_back(v):
    return v

def low_keep(v):
    return (low(v), None)

def low_pass(kept, grad):
    return (grad,)

def back_keep(v):
    return (v, None)

def back_low(kept, grad):
    return (low(grad),)
low.defvjp(low_keep, low_pass)
low_back.defvjp(back_keep, back_low)
norm_eps = 1e-06
masked_score = -1e+30
precise = lax.Precision.HIGHEST

def rotate(field, positions):
    half_width = field.shape[-1] // 2
    frequency = 10000.0 ** (-2.0 * jnp.arange(half_width, dtype=jnp.float32) / field.shape[-1])
    angles = positions.astype(jnp.float32)[:, None] * frequency[None, :]
    cos_part = jnp.cos(angles)[:, None, :]
    sin_part = jnp.sin(angles)[:, None, :]
    first_half = field[..., :half_width]
    second_half = field[..., half_width:]
    return jnp.concatenate([first_half * cos_part - second_half * sin_part, second_half * cos_part + first_half * sin_part], axis=-1)

def rms_scale(field):
    return lax.rsqrt(lax.optimization_barrier(jnp.mean(field * field, axis=-1, keepdims=True)) + norm_eps)

def attend(queries, key_rows, value_rows):
    groups = queries.shape[1] // key_rows.shape[1]
    query_block = min(512, queries.shape[0])
    block_count = queries.shape[0] // query_block
    key_pos = jnp.arange(key_rows.shape[0])

    def one_block(block_index):
        query_rows = lax.dynamic_slice_in_dim(queries, block_index * query_block, query_block, 0)
        query_rows = query_rows.reshape(query_block, key_rows.shape[1], groups, -1)
        scores = jnp.einsum('qgjd,kgd->gjqk', query_rows, key_rows, precision=precise) * query_rows.shape[-1] ** (-0.5)
        scores = low_back(scores)
        query_pos = block_index * query_block + jnp.arange(query_block)
        visible = (query_pos[:, None] >= key_pos[None, :])[None, None]
        scores = jnp.where(visible, scores, masked_score)
        probability = jax.nn.softmax(scores, axis=-1)
        result = jnp.einsum('gjqk,kgd->qgjd', low(probability), value_rows, precision=precise)
        return result.reshape(query_block, -1)
    results = lax.map(jax.checkpoint(one_block), jnp.arange(block_count))
    return results.reshape(queries.shape[0], -1)

def slot_tables(block_routes, block_gating):
    onehot = (block_routes[:, :, None] == jnp.arange(EXPERTS)[None, None, :]).astype(jnp.float32)
    flat_hot = onehot.reshape(-1, EXPERTS)
    before = jnp.cumsum(flat_hot, axis=0) - flat_hot
    rank_of = lax.optimization_barrier(jnp.sum(before * flat_hot, axis=-1)).reshape(block_routes.shape)
    slot_hot = (rank_of[:, :, None] == jnp.arange(CAP)[None, None, :]).astype(jnp.float32)
    picked = jnp.einsum('tke,tkc->ect', onehot, slot_hot, precision=precise)
    weighted = jnp.einsum('tke,tkc,tk->ect', onehot, slot_hot, block_gating, precision=precise)
    return (picked, weighted)

def block_forward(tok_field, tok_routes, weight_list):
    gain_one, gain_two, query_weight, key_weight, value_weight, out_weight, router_weight, gate_weight, up_weight, down_weight = weight_list
    positions = jnp.arange(LEN)
    normed = low(tok_field * rms_scale(tok_field) * gain_one)
    queries = low(rotate(low_back(jnp.dot(normed, query_weight, precision=precise)).reshape(LEN, HEADS, HD), positions))
    key_rows = low(rotate(low_back(jnp.dot(normed, key_weight, precision=precise)).reshape(LEN, KVH, HD), positions))
    value_rows = low(low_back(jnp.dot(normed, value_weight, precision=precise))).reshape(LEN, KVH, HD)
    attended = low(low_back(attend(queries, key_rows, value_rows)))
    hidden = tok_field + low_back(jnp.dot(attended, out_weight, precision=precise))
    normed_moe = low(hidden * rms_scale(hidden) * gain_two)
    logits = jnp.dot(normed_moe, router_weight, precision=precise)
    onehot = (tok_routes[:, :, None] == jnp.arange(EXPERTS)[None, None, :]).astype(jnp.float32)
    chosen = jnp.einsum('tke,te->tk', onehot, logits, precision=precise)
    gating = jax.nn.softmax(chosen, axis=-1)
    blocks = LEN // TOK_DEV

    def expert_block(inputs):
        block_rows, block_routes, block_gating = inputs
        picked, weighted = slot_tables(block_routes, block_gating)
        taken_rows = jnp.einsum('ect,td->ecd', picked, block_rows, precision=precise)
        gate_pre = low_back(jnp.einsum('ecd,edf->ecf', taken_rows, gate_weight, precision=precise))
        up_pre = low_back(jnp.einsum('ecd,edf->ecf', taken_rows, up_weight, precision=precise))
        activation = low(jax.nn.silu(gate_pre) * up_pre)
        expert_out = low_back(jnp.einsum('ecf,efd->ecd', activation, down_weight, precision=precise))
        return jnp.einsum('ect,ecd->td', weighted, expert_out, precision=precise)
    mixture = lax.map(jax.checkpoint(expert_block), (normed_moe.reshape(blocks, TOK_DEV, D), tok_routes.reshape(blocks, TOK_DEV, TOPK), gating.reshape(blocks, TOK_DEV, TOPK)))
    return hidden + mixture.reshape(LEN, D)

def reference(tokens, gain_attn, gain_moe, query_weight, key_weight, value_weight, out_weight, router_weight, gate_weight, up_weight, down_weight, expert_routes, cotangent):
    params = tuple((weight_arg.astype(jnp.float32) for weight_arg in (gain_attn, gain_moe, query_weight, key_weight, value_weight, out_weight, router_weight, gate_weight, up_weight, down_weight)))

    def forward_all(field_in, *weight_list):

        def one_sequence(carry, sequence):
            return (carry, block_forward(sequence[0], sequence[1], weight_list))
        final_carry, results = lax.scan(one_sequence, jnp.zeros((), jnp.float32), (field_in, expert_routes))
        return results
    result, pullback = jax.vjp(forward_all, tokens.astype(jnp.float32), *params)
    gradients = pullback(cotangent.astype(jnp.float32))
    return (result.astype(jnp.bfloat16), gradients[0].astype(jnp.bfloat16), gradients[1], gradients[2], gradients[3], gradients[4], gradients[5], gradients[6], gradients[7], gradients[8], gradients[9], gradients[10])
```

```python
import jax
import jax.numpy as jnp
from jax import lax
from jax.sharding import PartitionSpec as P

HD = 64


norm_eps = 1e-06
masked_score = -1e30
precise = lax.Precision.HIGHEST


def rotate(field, positions):
    half_width = field.shape[-1] // 2
    frequency = 10000.0 ** (-2.0 * jnp.arange(half_width, dtype=jnp.float32) / field.shape[-1])
    angles = positions.astype(jnp.float32)[:, None] * frequency[None, :]
    cos_part = jnp.cos(angles)[:, None, :]
    sin_part = jnp.sin(angles)[:, None, :]
    first_half = field[..., :half_width]
    second_half = field[..., half_width:]
    return jnp.concatenate(
        [
            first_half * cos_part - second_half * sin_part,
            second_half * cos_part + first_half * sin_part,
        ],
        axis=-1,
    )


def rotate_back(field, positions):
    half_width = field.shape[-1] // 2
    frequency = 10000.0 ** (-2.0 * jnp.arange(half_width, dtype=jnp.float32) / field.shape[-1])
    angles = positions.astype(jnp.float32)[:, None] * frequency[None, :]
    cos_part = jnp.cos(angles)[:, None, :]
    sin_part = jnp.sin(angles)[:, None, :]
    first_half = field[..., :half_width]
    second_half = field[..., half_width:]
    return jnp.concatenate(
        [
            first_half * cos_part + second_half * sin_part,
            second_half * cos_part - first_half * sin_part,
        ],
        axis=-1,
    )


def rms_scale(field):
    return lax.rsqrt(jnp.mean(field * field, axis=-1, keepdims=True) + norm_eps)


def norm_back(grad_normed, field, row_scale, gain_vec):
    grad_scaled = grad_normed * gain_vec
    grad_field = row_scale * grad_scaled - field * row_scale * row_scale * row_scale * jnp.mean(
        grad_scaled * field, axis=-1, keepdims=True
    )
    grad_gain = jnp.sum(grad_normed * field * row_scale, axis=0)
    return (grad_field, grad_gain)


def swap_tp(part):
    return lax.ppermute(part, "tp", [(0, 1), (1, 0)])


def sum_tp(part):
    low = part.astype(jnp.bfloat16)
    return low.astype(jnp.float32) + swap_tp(low).astype(jnp.float32)


def scatter_sum(grad, rows):
    parts = lax.psum_scatter(
        grad.reshape(lax.axis_size("shard"), lax.axis_size("ctx"), rows, grad.shape[1]),
        "shard",
        scatter_dimension=0,
        tiled=False,
    )
    return lax.psum_scatter(parts, "ctx", scatter_dimension=0, tiled=False)


def per_device(
    tokens,
    gain_attn,
    gain_moe,
    query_weight,
    key_weight,
    value_weight,
    out_weight,
    router_weight,
    gate_weight,
    up_weight,
    down_weight,
    expert_routes,
    cotangent,
):
    shards = lax.axis_size("shard")
    ctxs = lax.axis_size("ctx")
    shard_at = lax.axis_index("shard")
    ctx_at = lax.axis_index("ctx")
    tok_rows = tokens.shape[1]
    width = tokens.shape[2]
    expert_count = gate_weight.shape[0]
    own = expert_count // shards
    hidden_here = gate_weight.shape[2]
    width_here = gate_weight.shape[1]
    own_rows = width // (shards * ctxs)
    span = own * hidden_here
    positions = ctx_at * tok_rows + jnp.arange(tok_rows)

    q_cols = query_weight.shape[1]
    k_cols = key_weight.shape[1]
    full_qkv = lax.all_gather(
        jnp.concatenate([query_weight, key_weight, value_weight], axis=1),
        "shard", axis=0, tiled=True,
    )
    full_out = lax.all_gather(out_weight.T, "shard", axis=0, tiled=True)
    full_router = lax.all_gather(router_weight, "shard", axis=0, tiled=True)

    stacked = jnp.stack([gate_weight, up_weight, jnp.swapaxes(down_weight, 1, 2)], axis=0)
    stacked = stacked.reshape(3, shards, own, width_here, hidden_here).transpose(1, 3, 0, 2, 4)
    stacked = stacked.reshape(shards, width_here, 3 * span)
    expert_weights = lax.all_to_all(
        stacked, "shard", split_axis=0, concat_axis=0, tiled=True
    ).reshape(width, 3 * span)
    weight_gu = expert_weights[:, : 2 * span]
    weight_down = expert_weights[:, 2 * span :]
    chosen_here = jnp.sum(
        (expert_routes[0][:, :, None] == jnp.arange(expert_count)[None, None, :]).astype(
            jnp.float32
        ),
        axis=1,
    )
    chosen_all = lax.all_gather(chosen_here.astype(jnp.bfloat16), "shard", axis=0, tiled=True)
    cot_all = lax.all_gather(cotangent[0], "shard", axis=0, tiled=True)

    heads_here = q_cols // HD
    kv_here = k_cols // HD
    groups = heads_here // kv_here
    score_scale = HD ** (-0.5)
    tok_field = tokens[0].astype(jnp.float32)
    gain_one = gain_attn.astype(jnp.float32)
    gain_two = gain_moe.astype(jnp.float32)
    scale_one = rms_scale(tok_field)
    normed = (tok_field * scale_one * gain_one).astype(jnp.bfloat16)
    projected = jnp.dot(normed, full_qkv, preferred_element_type=jnp.float32)
    queries = rotate(
        projected[:, :q_cols].reshape(tok_rows, heads_here, HD), positions
    ).astype(jnp.bfloat16)
    key_rows = rotate(
        projected[:, q_cols : q_cols + k_cols].reshape(tok_rows, kv_here, HD), positions
    ).astype(jnp.bfloat16)
    value_rows = projected[:, q_cols + k_cols :].astype(jnp.bfloat16)
    kv_all = lax.all_gather(
        jnp.concatenate([key_rows.reshape(tok_rows, -1), value_rows], axis=1),
        "ctx", axis=0, tiled=True,
    )
    all_keys = kv_all[:, :k_cols].reshape(-1, kv_here, HD)
    all_values = kv_all[:, k_cols:].reshape(-1, kv_here, HD)
    grouped = queries.reshape(tok_rows, kv_here, groups, HD)
    key_pos = jnp.arange(all_keys.shape[0])
    visible = (positions[:, None] >= key_pos[None, :])[None, None]

    def masked_scores():
        raw_scores = (
            jnp.einsum("qgjd,kgd->gjqk", grouped, all_keys, preferred_element_type=jnp.float32)
            * score_scale
        )
        return jnp.where(visible, raw_scores, masked_score)

    scores = masked_scores()
    row_max = jnp.max(scores, axis=-1, keepdims=True)
    exp_vals = jnp.exp(scores - row_max)
    exp_total = jnp.sum(exp_vals, axis=-1, keepdims=True)
    probability_low = (exp_vals / exp_total).astype(jnp.bfloat16)
    log_total = row_max + jnp.log(exp_total)
    attended = (
        jnp.einsum(
            "gjqk,kgd->qgjd", probability_low, all_values, preferred_element_type=jnp.float32
        )
        .reshape(tok_rows, -1)
        .astype(jnp.bfloat16)
    )
    partial_attn = jnp.einsum(
        "th,dh->td", attended, full_out, preferred_element_type=jnp.float32
    )
    hidden = tok_field + sum_tp(partial_attn)
    scale_two = rms_scale(hidden)
    normed_moe = (hidden * scale_two * gain_two).astype(jnp.bfloat16)

    moe_all = lax.all_gather(normed_moe, "shard", axis=0, tiled=True)

    def gates(logits, chosen):
        shown = jnp.where(chosen > 0, logits, masked_score)
        weights = jnp.where(
            chosen > 0, jnp.exp(shown - jnp.max(shown, axis=-1, keepdims=True)), 0.0
        )
        return weights / jnp.sum(weights, axis=-1, keepdims=True)

    gates_all = gates(
        jnp.dot(moe_all, full_router, preferred_element_type=jnp.float32),
        chosen_all.astype(jnp.float32),
    )
    gates_own = lax.dynamic_slice_in_dim(gates_all, shard_at * own, own, 1)
    gate_up = jnp.dot(moe_all, weight_gu, preferred_element_type=jnp.float32)
    back_down = jnp.dot(cot_all, weight_down, preferred_element_type=jnp.float32)
    gates_wide = jnp.repeat(gates_own, hidden_here, axis=1)
    gate_pre = gate_up[:, :span]
    up_pre = gate_up[:, span:]
    sigmoid_gate = jax.nn.sigmoid(gate_pre)
    activation = (gate_pre * sigmoid_gate * up_pre).astype(jnp.bfloat16).astype(jnp.float32)
    gated_act = (gates_wide * activation).astype(jnp.bfloat16)
    grad_gates_part = jnp.sum(
        (activation * back_down).reshape(-1, own, hidden_here), axis=-1
    )
    grad_activation = gates_wide * back_down
    grad_gu = jnp.concatenate(
        [
            (
                grad_activation * up_pre * sigmoid_gate * (1.0 + gate_pre * (1.0 - sigmoid_gate))
            ).astype(jnp.bfloat16),
            (grad_activation * gate_pre * sigmoid_gate).astype(jnp.bfloat16),
        ],
        axis=1,
    )
    partial_moe = jnp.einsum(
        "tf,df->td", gated_act, weight_down, preferred_element_type=jnp.float32
    ).astype(jnp.bfloat16)
    grad_moe_part = jnp.einsum(
        "tf,df->td", grad_gu, weight_gu, preferred_element_type=jnp.float32
    ).astype(jnp.bfloat16)
    out_rows = lax.psum_scatter(partial_moe, "shard", scatter_dimension=0, tiled=True)
    grad_moe_rows = lax.psum_scatter(grad_moe_part, "shard", scatter_dimension=0, tiled=True)
    placed_gates = lax.dynamic_update_slice_in_dim(
        jnp.zeros((expert_count, shards * tok_rows), jnp.float32),
        grad_gates_part.T, shard_at * own, 0,
    )
    grad_gates = lax.psum_scatter(placed_gates, "shard", scatter_dimension=1, tiled=True)
    grad_gates = (grad_gates + swap_tp(grad_gates)).T

    gating = gates(
        jnp.dot(normed_moe, full_router, preferred_element_type=jnp.float32), chosen_here
    )
    grad_logits = gating * (grad_gates - jnp.sum(gating * grad_gates, axis=-1, keepdims=True))
    grad_normed_moe = sum_tp(grad_moe_rows) + jnp.einsum(
        "te,de->td", grad_logits, full_router.astype(jnp.float32)
    )
    grad_router_full = jnp.einsum(
        "td,te->ed", normed_moe.astype(jnp.float32), grad_logits
    )
    grad_out = cotangent[0].astype(jnp.float32)
    grad_hidden_norm, grad_gain_two = norm_back(grad_normed_moe, hidden, scale_two, gain_two)
    grad_hidden = grad_out + grad_hidden_norm
    grad_branch = grad_hidden.astype(jnp.bfloat16)
    grad_attended_flat = jnp.dot(
        grad_branch, full_out, preferred_element_type=jnp.float32
    ).astype(jnp.bfloat16)

    expert_grads = jnp.concatenate(
        [
            jnp.einsum("td,tf->df", moe_all, grad_gu, preferred_element_type=jnp.float32),
            jnp.einsum("td,tf->df", cot_all, gated_act, preferred_element_type=jnp.float32),
        ],
        axis=1,
    ).astype(jnp.bfloat16)
    expert_grads = expert_grads.reshape(shards, ctxs, own_rows, 3 * span).transpose(1, 0, 2, 3)
    expert_grads = lax.optimization_barrier(
        expert_grads.reshape(ctxs * shards * own_rows, 3 * span)
    )
    expert_grads = lax.psum_scatter(expert_grads, "ctx", scatter_dimension=0, tiled=True)
    expert_grads = lax.all_to_all(
        expert_grads.reshape(shards, own_rows, 3 * span), "shard", split_axis=0, concat_axis=0, tiled=True
    ).reshape(shards, own_rows, 3, own, hidden_here)
    expert_grads = expert_grads.astype(jnp.float32)
    grad_gate_own = expert_grads[:, :, 0].transpose(0, 2, 1, 3).reshape(
        expert_count, own_rows, hidden_here)
    grad_up_own = expert_grads[:, :, 1].transpose(0, 2, 1, 3).reshape(
        expert_count, own_rows, hidden_here)
    grad_down_own = expert_grads[:, :, 2].transpose(0, 2, 3, 1).reshape(
        expert_count, hidden_here, own_rows)

    result = hidden + sum_tp(out_rows)
    output = result.astype(jnp.bfloat16)[None]

    grad_out_full = jnp.einsum(
        "td,th->dh", grad_branch, attended, preferred_element_type=jnp.float32
    ).astype(jnp.bfloat16)
    grad_out_own = scatter_sum(grad_out_full, own_rows).astype(jnp.float32).T
    small = lax.psum(
        jnp.concatenate([grad_router_full, grad_gain_two[None]], axis=0), ("shard", "ctx")
    )
    small = lax.dynamic_slice_in_dim(small, (shard_at * ctxs + ctx_at) * own_rows, own_rows, 1)
    grad_router_own = small[:expert_count].T
    grad_gain_m = small[expert_count]
    grad_attended = grad_attended_flat.reshape(tok_rows, kv_here, groups, HD)
    probability_again = jnp.exp(masked_scores() - log_total)
    grad_probability = jnp.einsum(
        "qgjd,kgd->gjqk", grad_attended, all_values, preferred_element_type=jnp.float32
    )
    grad_values_all = jnp.einsum(
        "gjqk,qgjd->kgd",
        probability_again.astype(jnp.bfloat16),
        grad_attended,
        preferred_element_type=jnp.float32,
    )
    inner_sum = jnp.sum(probability_again * grad_probability, axis=-1, keepdims=True)
    grad_scores = (probability_again * (grad_probability - inner_sum)).astype(jnp.bfloat16)
    grad_queries = (
        jnp.einsum("gjqk,kgd->qgjd", grad_scores, all_keys, preferred_element_type=jnp.float32)
        * score_scale
    )
    grad_keys_all = (
        jnp.einsum("gjqk,qgjd->kgd", grad_scores, grouped, preferred_element_type=jnp.float32)
        * score_scale
    )
    grad_kv_all = jnp.concatenate(
        [
            grad_keys_all.reshape(-1, k_cols).astype(jnp.bfloat16),
            grad_values_all.reshape(-1, k_cols).astype(jnp.bfloat16),
        ],
        axis=1,
    )
    grad_kv = lax.psum_scatter(grad_kv_all, "ctx", scatter_dimension=0, tiled=True).astype(
        jnp.float32
    )
    grad_query_rows = (
        rotate_back(grad_queries.reshape(tok_rows, heads_here, HD), positions)
        .reshape(tok_rows, -1)
        .astype(jnp.bfloat16)
    )
    grad_key_rows = (
        rotate_back(grad_kv[:, :k_cols].reshape(tok_rows, kv_here, HD), positions)
        .reshape(tok_rows, -1)
        .astype(jnp.bfloat16)
    )
    grad_value_rows = grad_kv[:, k_cols:].astype(jnp.bfloat16)
    grad_rows = jnp.concatenate([grad_query_rows, grad_key_rows, grad_value_rows], axis=1)
    grad_normed_part = jnp.einsum(
        "th,dh->td", grad_rows, full_qkv, preferred_element_type=jnp.float32
    )
    grad_normed = sum_tp(grad_normed_part)
    grad_qkv_full = jnp.einsum(
        "td,th->dh", normed, grad_rows, preferred_element_type=jnp.float32
    ).astype(jnp.bfloat16)
    grad_qkv_own = scatter_sum(grad_qkv_full, own_rows).astype(jnp.float32)
    grad_field_norm, _ = norm_back(grad_normed, tok_field, scale_one, gain_one)
    grad_gain_one = lax.psum(
        jnp.sum(grad_normed_part * tok_field * scale_one, axis=0), ("shard", "ctx", "tp")
    )
    grad_gain_a = lax.dynamic_slice_in_dim(
        grad_gain_one, (shard_at * ctxs + ctx_at) * own_rows, own_rows, 0
    )
    grad_tokens = (grad_hidden + grad_field_norm).astype(jnp.bfloat16)[None]
    return (
        output,
        grad_tokens,
        grad_gain_a,
        grad_gain_m,
        grad_qkv_own[:, :q_cols],
        grad_qkv_own[:, q_cols : q_cols + k_cols],
        grad_qkv_own[:, q_cols + k_cols :],
        grad_out_own,
        grad_router_own,
        grad_gate_own,
        grad_up_own,
        grad_down_own,
    )


def solution(mesh):
    placed = (
        P("shard", "ctx", None),
        P(),
        P(),
        P("shard", "tp"),
        P("shard", "tp"),
        P("shard", "tp"),
        P("tp", "shard"),
        P("shard", None),
        P(None, "shard", "tp"),
        P(None, "shard", "tp"),
        P(None, "tp", "shard"),
        P("shard", "ctx", None),
        P("shard", "ctx", None),
    )
    return jax.shard_map(
        per_device,
        mesh=mesh,
        in_specs=placed,
        out_specs=(
            P("shard", "ctx", None),
            P("shard", "ctx", None),
            P(("shard", "ctx")),
            P(("shard", "ctx")),
            P(("shard", "ctx"), "tp"),
            P(("shard", "ctx"), "tp"),
            P(("shard", "ctx"), "tp"),
            P("tp", ("shard", "ctx")),
            P(("shard", "ctx"), None),
            P(None, ("shard", "ctx"), "tp"),
            P(None, ("shard", "ctx"), "tp"),
            P(None, "tp", ("shard", "ctx")),
        ),
        check_vma=False,
    )
```

```python
import jax
import jax.numpy as jnp
from jax import lax
from jax.sharding import PartitionSpec as P

HD = 64


norm_eps = 1e-06
masked_score = -1e30
precise = lax.Precision.HIGHEST


def rotate(field, positions):
    half_width = field.shape[-1] // 2
    frequency = 10000.0 ** (-2.0 * jnp.arange(half_width, dtype=jnp.float32) / field.shape[-1])
    angles = positions.astype(jnp.float32)[:, None] * frequency[None, :]
    cos_part = jnp.cos(angles)[:, None, :]
    sin_part = jnp.sin(angles)[:, None, :]
    first_half = field[..., :half_width]
    second_half = field[..., half_width:]
    return jnp.concatenate(
        [
            first_half * cos_part - second_half * sin_part,
            second_half * cos_part + first_half * sin_part,
        ],
        axis=-1,
    )


def rotate_back(field, positions):
    half_width = field.shape[-1] // 2
    frequency = 10000.0 ** (-2.0 * jnp.arange(half_width, dtype=jnp.float32) / field.shape[-1])
    angles = positions.astype(jnp.float32)[:, None] * frequency[None, :]
    cos_part = jnp.cos(angles)[:, None, :]
    sin_part = jnp.sin(angles)[:, None, :]
    first_half = field[..., :half_width]
    second_half = field[..., half_width:]
    return jnp.concatenate(
        [
            first_half * cos_part + second_half * sin_part,
            second_half * cos_part - first_half * sin_part,
        ],
        axis=-1,
    )


def rms_scale(field):
    return lax.rsqrt(jnp.mean(field * field, axis=-1, keepdims=True) + norm_eps)


def norm_back(grad_normed, field, row_scale, gain_vec):
    grad_scaled = grad_normed * gain_vec
    grad_field = row_scale * grad_scaled - field * row_scale * row_scale * row_scale * jnp.mean(
        grad_scaled * field, axis=-1, keepdims=True
    )
    grad_gain = jnp.sum(grad_normed * field * row_scale, axis=0)
    return (grad_field, grad_gain)


def swap_tp(part):
    return lax.ppermute(part, "tp", [(0, 1), (1, 0)])


def sum_tp(part):
    low = part.astype(jnp.bfloat16)
    return low.astype(jnp.float32) + swap_tp(low).astype(jnp.float32)


def widen(cols):
    return jnp.pad(cols, ((0, 0), (0, 128 - cols.shape[1])))


def exchange(blocks):
    count = lax.axis_size("shard")
    at = lax.axis_index("shard")
    own_block = lax.dynamic_slice_in_dim(blocks, at, 1, 0)
    arrived = lax.dynamic_update_slice_in_dim(jnp.zeros_like(blocks), own_block, at, 0)
    for shift in range(1, count):
        sent = lax.dynamic_slice_in_dim(blocks, (at + shift) % count, 1, 0)
        got = lax.ppermute(sent, "shard", [(i, (i + shift) % count) for i in range(count)])
        arrived = lax.dynamic_update_slice_in_dim(arrived, got, (at - shift) % count, 0)
    return arrived


def scatter_sum(grad, rows):
    parts = lax.psum_scatter(
        grad.reshape(lax.axis_size("shard"), lax.axis_size("ctx"), rows, grad.shape[1]),
        "shard",
        scatter_dimension=0,
        tiled=False,
    )
    return lax.psum_scatter(parts, "ctx", scatter_dimension=0, tiled=False)


def per_device(
    tokens,
    gain_attn,
    gain_moe,
    query_weight,
    key_weight,
    value_weight,
    out_weight,
    router_weight,
    gate_weight,
    up_weight,
    down_weight,
    expert_routes,
    cotangent,
):
    shards = lax.axis_size("shard")
    ctxs = lax.axis_size("ctx")
    shard_at = lax.axis_index("shard")
    ctx_at = lax.axis_index("ctx")
    tok_rows = tokens.shape[1]
    width = tokens.shape[2]
    expert_count = gate_weight.shape[0]
    own = expert_count // shards
    hidden_here = gate_weight.shape[2]
    width_here = gate_weight.shape[1]
    own_rows = width // (shards * ctxs)
    span = own * hidden_here
    positions = ctx_at * tok_rows + jnp.arange(tok_rows)

    q_cols = query_weight.shape[1]
    k_cols = key_weight.shape[1]
    full_qkv = lax.all_gather(
        jnp.concatenate([query_weight, key_weight, value_weight], axis=1),
        "shard", axis=0, tiled=True,
    )
    head_cols = out_weight.shape[0]
    out_router = lax.all_gather(
        jnp.concatenate([out_weight.T, widen(router_weight)], axis=1),
        "shard", axis=0, tiled=True,
    )
    full_out = out_router[:, :head_cols]
    full_router = out_router[:, head_cols : head_cols + expert_count]

    stacked = jnp.stack([gate_weight, up_weight, jnp.swapaxes(down_weight, 1, 2)], axis=0)
    stacked = stacked.reshape(3, shards, own, width_here, hidden_here).transpose(1, 3, 0, 2, 4)
    stacked = stacked.reshape(shards, width_here, 3 * span)
    expert_weights = exchange(stacked).reshape(width, 3 * span)
    weight_gu = expert_weights[:, : 2 * span]
    weight_down = expert_weights[:, 2 * span :]
    chosen_here = jnp.sum(
        (expert_routes[0][:, :, None] == jnp.arange(expert_count)[None, None, :]).astype(
            jnp.float32
        ),
        axis=1,
    )
    cot_chosen = lax.all_gather(
        jnp.concatenate([cotangent[0], widen(chosen_here.astype(jnp.bfloat16))], axis=1),
        "shard", axis=0, tiled=True,
    )
    cot_all = cot_chosen[:, :width]
    chosen_all = cot_chosen[:, width : width + expert_count]

    heads_here = q_cols // HD
    kv_here = k_cols // HD
    groups = heads_here // kv_here
    score_scale = HD ** (-0.5)
    tok_field = tokens[0].astype(jnp.float32)
    gain_one = gain_attn.astype(jnp.float32)
    gain_two = gain_moe.astype(jnp.float32)
    scale_one = rms_scale(tok_field)
    normed = (tok_field * scale_one * gain_one).astype(jnp.bfloat16)
    projected = jnp.dot(normed, full_qkv, preferred_element_type=jnp.float32)
    queries = rotate(
        projected[:, :q_cols].reshape(tok_rows, heads_here, HD), positions
    ).astype(jnp.bfloat16)
    key_rows = rotate(
        projected[:, q_cols : q_cols + k_cols].reshape(tok_rows, kv_here, HD), positions
    ).astype(jnp.bfloat16)
    value_rows = projected[:, q_cols + k_cols :].astype(jnp.bfloat16)
    kv_all = lax.all_gather(
        jnp.concatenate([key_rows.reshape(tok_rows, -1), value_rows], axis=1),
        "ctx", axis=0, tiled=True,
    )
    all_keys = kv_all[:, :k_cols].reshape(-1, kv_here, HD)
    all_values = kv_all[:, k_cols:].reshape(-1, kv_here, HD)
    grouped = queries.reshape(tok_rows, kv_here, groups, HD)
    key_pos = jnp.arange(all_keys.shape[0])
    visible = (positions[:, None] >= key_pos[None, :])[None, None]

    def masked_scores():
        raw_scores = (
            jnp.einsum("qgjd,kgd->gjqk", grouped, all_keys, preferred_element_type=jnp.float32)
            * score_scale
        )
        return jnp.where(visible, raw_scores, masked_score)

    scores = masked_scores()
    row_max = jnp.max(scores, axis=-1, keepdims=True)
    exp_vals = jnp.exp(scores - row_max)
    exp_total = jnp.sum(exp_vals, axis=-1, keepdims=True)
    probability_low = (exp_vals / exp_total).astype(jnp.bfloat16)
    log_total = row_max + jnp.log(exp_total)
    attended = (
        jnp.einsum(
            "gjqk,kgd->qgjd", probability_low, all_values, preferred_element_type=jnp.float32
        )
        .reshape(tok_rows, -1)
        .astype(jnp.bfloat16)
    )
    partial_attn = jnp.einsum(
        "th,dh->td", attended, full_out, preferred_element_type=jnp.float32
    )
    hidden = tok_field + sum_tp(partial_attn)
    scale_two = rms_scale(hidden)
    normed_moe = (hidden * scale_two * gain_two).astype(jnp.bfloat16)

    moe_all = lax.all_gather(normed_moe, "shard", axis=0, tiled=True)

    def gates(logits, chosen):
        shown = jnp.where(chosen > 0, logits, masked_score)
        weights = jnp.where(
            chosen > 0, jnp.exp(shown - jnp.max(shown, axis=-1, keepdims=True)), 0.0
        )
        return weights / jnp.sum(weights, axis=-1, keepdims=True)

    gates_all = gates(
        jnp.dot(moe_all, full_router, preferred_element_type=jnp.float32),
        chosen_all.astype(jnp.float32),
    )
    gates_own = lax.dynamic_slice_in_dim(gates_all, shard_at * own, own, 1)
    gate_up = jnp.dot(moe_all, weight_gu, preferred_element_type=jnp.float32)
    back_down = jnp.dot(cot_all, weight_down, preferred_element_type=jnp.float32)
    gates_wide = jnp.repeat(gates_own, hidden_here, axis=1)
    gate_pre = gate_up[:, :span]
    up_pre = gate_up[:, span:]
    sigmoid_gate = jax.nn.sigmoid(gate_pre)
    activation = (gate_pre * sigmoid_gate * up_pre).astype(jnp.bfloat16).astype(jnp.float32)
    gated_act = (gates_wide * activation).astype(jnp.bfloat16)
    grad_gates_part = jnp.sum(
        (activation * back_down).reshape(-1, own, hidden_here), axis=-1
    )
    grad_activation = gates_wide * back_down
    grad_gu = jnp.concatenate(
        [
            (
                grad_activation * up_pre * sigmoid_gate * (1.0 + gate_pre * (1.0 - sigmoid_gate))
            ).astype(jnp.bfloat16),
            (grad_activation * gate_pre * sigmoid_gate).astype(jnp.bfloat16),
        ],
        axis=1,
    )
    partial_moe = jnp.einsum(
        "tf,df->td", gated_act, weight_down, preferred_element_type=jnp.float32
    ).astype(jnp.bfloat16)
    grad_moe_part = jnp.einsum(
        "tf,df->td", grad_gu, weight_gu, preferred_element_type=jnp.float32
    ).astype(jnp.bfloat16)
    placed_gates = lax.dynamic_update_slice_in_dim(
        jnp.zeros((shards * tok_rows, 128), jnp.bfloat16),
        grad_gates_part.astype(jnp.bfloat16), shard_at * own, 1,
    )
    back_rows = lax.psum_scatter(
        jnp.concatenate([grad_moe_part, placed_gates], axis=1),
        "shard", scatter_dimension=0, tiled=True,
    )
    expert_grads = jnp.concatenate(
        [
            jnp.einsum("td,tf->df", moe_all, grad_gu, preferred_element_type=jnp.float32),
            jnp.einsum("td,tf->df", cot_all, gated_act, preferred_element_type=jnp.float32),
        ],
        axis=1,
    ).astype(jnp.bfloat16)
    expert_grads = expert_grads.reshape(shards, ctxs, own_rows, 3 * span).transpose(1, 0, 2, 3)
    back_rows, expert_grads = lax.optimization_barrier(
        (back_rows, expert_grads.reshape(ctxs * shards * own_rows, 3 * span))
    )
    back_sum = sum_tp(back_rows)
    grad_gates = back_sum[:, width : width + expert_count]

    gating = gates(
        jnp.dot(normed_moe, full_router, preferred_element_type=jnp.float32), chosen_here
    )
    grad_logits = gating * (grad_gates - jnp.sum(gating * grad_gates, axis=-1, keepdims=True))
    grad_normed_moe = back_sum[:, :width] + jnp.einsum(
        "te,de->td", grad_logits, full_router.astype(jnp.float32)
    )
    grad_router_full = jnp.einsum(
        "td,te->de", normed_moe.astype(jnp.float32), grad_logits
    )
    grad_out = cotangent[0].astype(jnp.float32)
    grad_hidden_norm, grad_gain_two = norm_back(grad_normed_moe, hidden, scale_two, gain_two)
    grad_hidden = grad_out + grad_hidden_norm
    grad_branch = grad_hidden.astype(jnp.bfloat16)
    grad_attended_flat = jnp.dot(
        grad_branch, full_out, preferred_element_type=jnp.float32
    ).astype(jnp.bfloat16)

    grad_attended_flat, partial_moe = lax.optimization_barrier((grad_attended_flat, partial_moe))
    out_rows = lax.psum_scatter(partial_moe, "shard", scatter_dimension=0, tiled=True)
    expert_grads = lax.psum_scatter(expert_grads, "ctx", scatter_dimension=0, tiled=True)
    expert_grads = exchange(expert_grads.reshape(shards, own_rows, 3 * span)).reshape(shards, own_rows, 3, own, hidden_here)
    expert_grads = expert_grads.astype(jnp.float32)
    grad_gate_own = expert_grads[:, :, 0].transpose(0, 2, 1, 3).reshape(
        expert_count, own_rows, hidden_here)
    grad_up_own = expert_grads[:, :, 1].transpose(0, 2, 1, 3).reshape(
        expert_count, own_rows, hidden_here)
    grad_down_own = expert_grads[:, :, 2].transpose(0, 2, 3, 1).reshape(
        expert_count, hidden_here, own_rows)

    result = hidden + sum_tp(out_rows)
    output = result.astype(jnp.bfloat16)[None]

    grad_out_full = jnp.einsum(
        "td,th->dh", grad_branch, attended, preferred_element_type=jnp.float32
    ).astype(jnp.bfloat16)
    extra = jnp.concatenate([grad_router_full, grad_gain_two[:, None]], axis=1)
    grad_out_own = scatter_sum(
        jnp.concatenate([grad_out_full, widen(extra.astype(jnp.bfloat16))], axis=1), own_rows
    ).astype(jnp.float32)
    grad_router_own = grad_out_own[:, head_cols : head_cols + expert_count]
    grad_gain_m = grad_out_own[:, head_cols + expert_count]
    grad_out_own = grad_out_own[:, :head_cols].T
    grad_attended = grad_attended_flat.reshape(tok_rows, kv_here, groups, HD)
    probability_again = jnp.exp(masked_scores() - log_total)
    grad_probability = jnp.einsum(
        "qgjd,kgd->gjqk", grad_attended, all_values, preferred_element_type=jnp.float32
    )
    grad_values_all = jnp.einsum(
        "gjqk,qgjd->kgd",
        probability_again.astype(jnp.bfloat16),
        grad_attended,
        preferred_element_type=jnp.float32,
    )
    inner_sum = jnp.sum(probability_again * grad_probability, axis=-1, keepdims=True)
    grad_scores = (probability_again * (grad_probability - inner_sum)).astype(jnp.bfloat16)
    grad_queries = (
        jnp.einsum("gjqk,kgd->qgjd", grad_scores, all_keys, preferred_element_type=jnp.float32)
        * score_scale
    )
    grad_keys_all = (
        jnp.einsum("gjqk,qgjd->kgd", grad_scores, grouped, preferred_element_type=jnp.float32)
        * score_scale
    )
    grad_kv_all = jnp.concatenate(
        [
            grad_keys_all.reshape(-1, k_cols).astype(jnp.bfloat16),
            grad_values_all.reshape(-1, k_cols).astype(jnp.bfloat16),
        ],
        axis=1,
    )
    grad_kv = lax.psum_scatter(grad_kv_all, "ctx", scatter_dimension=0, tiled=True).astype(
        jnp.float32
    )
    grad_query_rows = (
        rotate_back(grad_queries.reshape(tok_rows, heads_here, HD), positions)
        .reshape(tok_rows, -1)
        .astype(jnp.bfloat16)
    )
    grad_key_rows = (
        rotate_back(grad_kv[:, :k_cols].reshape(tok_rows, kv_here, HD), positions)
        .reshape(tok_rows, -1)
        .astype(jnp.bfloat16)
    )
    grad_value_rows = grad_kv[:, k_cols:].astype(jnp.bfloat16)
    grad_rows = jnp.concatenate([grad_query_rows, grad_key_rows, grad_value_rows], axis=1)
    grad_normed_part = jnp.einsum(
        "th,dh->td", grad_rows, full_qkv, preferred_element_type=jnp.float32
    )
    grad_normed = sum_tp(grad_normed_part)
    grad_qkv_full = jnp.einsum(
        "td,th->dh", normed, grad_rows, preferred_element_type=jnp.float32
    ).astype(jnp.bfloat16)
    gain_one_part = jnp.sum(grad_normed_part * tok_field * scale_one, axis=0)[:, None]
    grad_qkv_own = scatter_sum(
        jnp.concatenate([grad_qkv_full, widen(gain_one_part.astype(jnp.bfloat16))], axis=1),
        own_rows,
    )
    grad_gain_a = sum_tp(grad_qkv_own[:, q_cols + 2 * k_cols :])[:, 0]
    grad_qkv_own = grad_qkv_own[:, : q_cols + 2 * k_cols].astype(jnp.float32)
    grad_field_norm, _ = norm_back(grad_normed, tok_field, scale_one, gain_one)
    grad_tokens = (grad_hidden + grad_field_norm).astype(jnp.bfloat16)[None]
    return (
        output,
        grad_tokens,
        grad_gain_a,
        grad_gain_m,
        grad_qkv_own[:, :q_cols],
        grad_qkv_own[:, q_cols : q_cols + k_cols],
        grad_qkv_own[:, q_cols + k_cols :],
        grad_out_own,
        grad_router_own,
        grad_gate_own,
        grad_up_own,
        grad_down_own,
    )


def solution(mesh):
    placed = (
        P("shard", "ctx", None),
        P(),
        P(),
        P("shard", "tp"),
        P("shard", "tp"),
        P("shard", "tp"),
        P("tp", "shard"),
        P("shard", None),
        P(None, "shard", "tp"),
        P(None, "shard", "tp"),
        P(None, "tp", "shard"),
        P("shard", "ctx", None),
        P("shard", "ctx", None),
    )
    return jax.shard_map(
        per_device,
        mesh=mesh,
        in_specs=placed,
        out_specs=(
            P("shard", "ctx", None),
            P("shard", "ctx", None),
            P(("shard", "ctx")),
            P(("shard", "ctx")),
            P(("shard", "ctx"), "tp"),
            P(("shard", "ctx"), "tp"),
            P(("shard", "ctx"), "tp"),
            P("tp", ("shard", "ctx")),
            P(("shard", "ctx"), None),
            P(None, ("shard", "ctx"), "tp"),
            P(None, ("shard", "ctx"), "tp"),
            P(None, "tp", ("shard", "ctx")),
        ),
        check_vma=False,
    )
```
